32 devices in a mesh: ctx: 4 (over y, x), exp: 8 (over z, core).
Axes of the slice: x: 2, y: 2, z: 4, core: 2. Of those that a mesh axis runs over, the one named last changes fastest.
Arguments:
- residual: bfloat16 [4096, 2048], P(('ctx', 'exp')), may hold values from -6 to 6
- queries: bfloat16 [4096, 4096], P('ctx', 'exp'), may hold values from -6.5 to 6.5
- key_rows: bfloat16 [4096, 512], P('ctx'), may hold values from -6.5 to 6.5
- value_rows: bfloat16 [4096, 512], P('ctx'), may hold values from -6 to 6
- segment_ids: int32 [4096], P('ctx'), may hold values from 0 to 15, never falling along the last dimension, each value on 1 to 2304 neighbouring positions
- out_weight: bfloat16 [4096, 2048], P('exp'), may hold values from -0.09375 to 0.09375
- norm_gain: float32 [2048], replicated, may hold values from 0.5 to 1.5
- expert_ids: int32 [4096, 8], P(('ctx', 'exp')), may hold values from 0 to 31, all different within a row; in each aligned block of 128 rows (0 to 127, 128 to 255, ...) at most 64 rows name the same one
- route_weight: float32 [4096, 8], P(('ctx', 'exp')), may hold values from 0.02 to 0.3
- gate_weight: bfloat16 [32, 2048, 768], P(('ctx', 'exp')), may hold values from -0.125 to 0.125
- up_weight: bfloat16 [32, 2048, 768], P(('ctx', 'exp')), may hold values from -0.125 to 0.125
- down_weight: bfloat16 [32, 768, 2048], P(('ctx', 'exp')), may hold values from -0.21875 to 0.21875
Outputs:
- layer_out: bfloat16 [4096, 2048], P(('ctx', 'exp'))
The draws below stay inside these ranges and needn't reach their ends.
Inputs may be any that keep to these rules, and one draw needn't show every extreme that they name: `expert_ids`: within the rows of one device (128 aligned positions), no expert is named by more than 64 rows; some expert is named by exactly 64. `segment_ids`: never falling along positions; each segment covers at most 2304 positions, and some segment exactly 2304.
All inputs are finite; a program needn't handle non-finite values.
Results may differ from the reference program's by a relative error of at most 0.013.
Values may be sent and summed in bfloat16 or wider, within the bound.
A program may use at most 128 MiB of HBM per device.

```python
import math
import jax
import jax.numpy as jnp
import numpy as np
from jax import lax

D = 2048
HEADS = 32
KV_HEADS = 4
HEAD_DIM = 128
FF_EXP = 768
TOP = 8
ROWS_DEV = 128
HEADS_DEV = 4
LENGTH = 4096
SEG_MOST = 2304
EXPERTS = 32
CAP = 64
SEGS = 16
N_CTX = 4
N_EXP = 8


def draw_queries(key, part):
    fresh_key = jax.random.fold_in(key, 1)
    return jnp.clip(jax.random.normal(fresh_key, (LENGTH, HEADS * HEAD_DIM), jnp.float32), -6.5, 6.5).astype(jnp.bfloat16)


def draw_key_rows(key, part):
    fresh_key = jax.random.fold_in(key, 2)
    return jnp.clip(jax.random.normal(fresh_key, (LENGTH, KV_HEADS * HEAD_DIM), jnp.float32), -6.5, 6.5).astype(jnp.bfloat16)


def shard_levels(key, extent, pieces, smallest, top_value):
    def one(axis_at, parts):
        draws = jax.random.uniform(jax.random.fold_in(jax.random.fold_in(key, 6), axis_at), (parts,), jnp.float32, smallest / len(pieces), top_value / len(pieces))
        return jnp.repeat(jnp.exp(draws), extent[axis_at] // parts).reshape((-1,) + (1,) * (len(extent) - axis_at - 1))

    loudness = one(*pieces[0])
    for cut in pieces[1:]:
        loudness = loudness * one(*cut)
    return loudness


def split_up(number_of, total, reach, skew):
    weights = [(1 << 20) // math.isqrt(standing ** skew) + 1 for standing in range(2, number_of + 1)]
    rest, given = total - reach - (number_of - 1), [1] * (number_of - 1)
    while rest > 0:
        candidates = [i for i in range(number_of - 1) if given[i] < reach]
        whole, budget = sum([weights[i] for i in candidates]), rest
        for i in candidates:
            addition = min(reach - given[i], max(1, budget * weights[i] // whole), rest)
            given[i] = given[i] + addition
            rest = rest - addition
    return np.array([reach] + given)


def ragged(stream_key, count, total, most, skew):
    if count == 2:
        one = jax.random.randint(stream_key, (), max(1, total - most), min(most, total - 1) + 1)
        return jnp.stack([one, total - one])
    sizes = jnp.asarray(split_up(count, total, most, skew), jnp.int32)
    twos = (count - 1) // 2
    donor, sink = sizes[1:1 + 2 * twos:2], sizes[2:2 + 2 * twos:2]
    slack = jnp.minimum(donor - 1, most - sink)
    shifted = jax.random.randint(jax.random.fold_in(stream_key, 1), (twos,), 0, 1 << 20) % (slack + 1)
    sizes = sizes.at[1:1 + 2 * twos:2].set(donor - shifted).at[2:2 + 2 * twos:2].set(sink + shifted)
    return sizes[jax.random.permutation(jax.random.fold_in(stream_key, 2), count)]


def assign_block(own_key, own, number, rows, count, top, limit, skew):
    sequence = jax.random.permutation(own_key, count)
    heavy_load, usual = shares(count, rows * top, limit, skew, True), shares(count, rows * top, limit, skew, False)
    places = jnp.arange(count)

    def named(sizes, offset_by):
        used = int((sizes > 0).sum())
        fixed = max(1, used // 4)
        moved = fixed + (places - fixed + offset_by * (used - fixed)) % max(1, count - fixed)
        return jnp.zeros((count,), jnp.int32).at[sequence[jnp.where(places < fixed, places, moved)]].set(jnp.asarray(sizes, jnp.int32))

    sizes = jnp.where(number % 4 == 0, named(heavy_load, number // 4), named(usual, number - number // 4 - 1))
    mixed = jax.random.permutation(jax.random.fold_in(own, 3), count)
    giver, taker = mixed[0:count // 2 * 2:2], mixed[1:count // 2 * 2:2]
    slack = jnp.minimum(sizes[giver] - 1, limit - sizes[taker]) // 2
    slack = jnp.where((giver == sequence[0]) | (taker == sequence[0]) | (sizes[taker] == 0), 0, jnp.maximum(slack, 0))
    moved = jax.random.randint(jax.random.fold_in(own, 4), (count // 2,), 0, 1 << 20) % (slack + 1)
    sizes = sizes.at[giver].add(-moved).at[taker].add(moved)
    labels = jnp.searchsorted(jnp.cumsum(sizes), jnp.arange(rows * top), side="right").astype(jnp.int32)
    listing = labels.reshape(top, rows).T
    listing = listing[jax.random.permutation(jax.random.fold_in(own, 1), rows)]
    offset_by = jax.random.randint(jax.random.fold_in(own, 2), (rows, 1), 0, top)
    return jnp.take_along_axis(listing, (jnp.arange(top)[None, :] + offset_by) % top, axis=1)


def shares(count, total, limit, skew, full):
    weights = [(1 << 20) // math.isqrt(grade ** skew) + 1 for grade in range(1, count + 1)]
    largest = limit if full else min(limit, max(-(-total // count), total * weights[0] // sum(weights)))
    least = 1 if total - largest >= count - 1 else 0
    given, surplus = [largest] + [least] * (count - 1), total - largest - least * (count - 1)
    while surplus > 0:
        free = [i for i in range(1, count) if given[i] < largest] or [i for i in range(1, count) if given[i] < limit]
        mass, budget = sum([weights[i] for i in free]), surplus
        for i in free:
            more = min(limit - given[i], max(1, budget * weights[i] // mass), surplus)
            given[i] = given[i] + more
            surplus = surplus - more
    return np.array(given)


def normal_values(own_key, extent, deviation, limit, cuts=(), held_as=jnp.bfloat16):
    factor_of = shard_levels(own_key, extent, cuts, -0.22, 0.18) if cuts else 1.0
    values = jax.random.normal(own_key, extent, jnp.float32) * deviation * factor_of
    return jnp.minimum(jnp.maximum(values, -limit), limit).astype(held_as)


def setup_inputs(seed: int = 0) -> dict:
    streams_of = jax.random.split(jax.random.key(seed), 13)
    residual = normal_values(streams_of[0], (LENGTH, D), 1.0, 6.0, ((0, 32),))
    queries = draw_queries(jax.random.fold_in(streams_of[12], 71), 0)
    key_rows = draw_key_rows(jax.random.fold_in(streams_of[12], 71), 0)
    value_rows = normal_values(streams_of[3], (LENGTH, KV_HEADS * HEAD_DIM), 1.0, 6.0, ((0, 4),))
    segment_ids = jnp.searchsorted(jnp.cumsum(ragged(streams_of[4], SEGS, LENGTH, SEG_MOST, 2)), jnp.arange(LENGTH), side="right").astype(jnp.int32)
    out_weight = normal_values(streams_of[5], (HEADS * HEAD_DIM, D), (HEADS * HEAD_DIM) ** -0.5, 0.09375, ((0, 8),))
    norm_gain = jnp.clip(1.0 + 0.1 * jax.random.normal(streams_of[6], (D,), jnp.float32), 0.5, 1.5)
    expert_ids_keys = jax.random.split(jax.random.fold_in(streams_of[7], 1), LENGTH // ROWS_DEV)
    expert_ids_turns = jax.random.permutation(jax.random.fold_in(streams_of[7], 3), LENGTH // ROWS_DEV)
    expert_ids = jax.vmap(lambda own, number: assign_block(jax.random.fold_in(streams_of[7], 2), own, number, ROWS_DEV, EXPERTS, TOP, CAP, 1))(expert_ids_keys, expert_ids_turns).reshape((LENGTH, TOP))
    route_weight = jnp.clip(0.02 + 0.28 * jax.random.uniform(streams_of[8], (LENGTH, TOP), jnp.float32) ** shard_levels(streams_of[8], (LENGTH, TOP), ((0, 32),), -0.2, 0.2), 0.02, 0.3)
    gate_weight = normal_values(streams_of[9], (EXPERTS, D, FF_EXP), D ** -0.5, 0.125, ((0, 32),))
    up_weight = normal_values(streams_of[10], (EXPERTS, D, FF_EXP), D ** -0.5, 0.125, ((0, 32),))
    down_weight = normal_values(streams_of[11], (EXPERTS, FF_EXP, D), FF_EXP ** -0.5, 0.21875, ((0, 32),))
    return dict(residual=residual, queries=queries, key_rows=key_rows, value_rows=value_rows, segment_ids=segment_ids, out_weight=out_weight, norm_gain=norm_gain, expert_ids=expert_ids, route_weight=route_weight, gate_weight=gate_weight, up_weight=up_weight, down_weight=down_weight)


def reference(residual, queries, key_rows, value_rows, segment_ids, out_weight, norm_gain, expert_ids, route_weight, gate_weight, up_weight, down_weight):
    group_size = HEADS // KV_HEADS
    block_rows = min(512, LENGTH)
    window = SEG_MOST + block_rows
    score_scale = 1.0 / math.sqrt(HEAD_DIM)
    key_padded = jnp.concatenate([jnp.zeros((SEG_MOST, KV_HEADS * HEAD_DIM), jnp.bfloat16), key_rows], 0)
    value_padded = jnp.concatenate([jnp.zeros((SEG_MOST, KV_HEADS * HEAD_DIM), jnp.bfloat16), value_rows], 0)
    seg_padded = jnp.concatenate([jnp.full((SEG_MOST,), -1, jnp.int32), segment_ids.astype(jnp.int32)], 0)

    def attend_block(block_index):
        query_start = (block_index * block_rows).astype(jnp.int32)
        query_block = lax.dynamic_slice_in_dim(queries, query_start, block_rows, 0).astype(jnp.float32)
        query_block = query_block.reshape(block_rows, KV_HEADS, group_size, HEAD_DIM)
        key_block = lax.dynamic_slice_in_dim(key_padded, query_start, window, 0).astype(jnp.float32).reshape(window, KV_HEADS, HEAD_DIM)
        value_block = lax.dynamic_slice_in_dim(value_padded, query_start, window, 0).astype(jnp.float32).reshape(window, KV_HEADS, HEAD_DIM)
        key_segs = lax.dynamic_slice_in_dim(seg_padded, query_start, window, 0)
        query_segs = lax.dynamic_slice_in_dim(segment_ids.astype(jnp.int32), query_start, block_rows, 0)
        query_pos = query_start + jnp.arange(block_rows, dtype=jnp.int32)
        key_pos = query_start - SEG_MOST + jnp.arange(window, dtype=jnp.int32)
        visible = (query_segs[:, None] == key_segs[None, :]) & (key_pos[None, :] <= query_pos[:, None])
        scores = jnp.einsum('qkgd,wkd->kgqw', query_block, key_block) * score_scale
        scores = jnp.where(visible[None, None], scores, -jnp.inf)
        row_max = lax.optimization_barrier(jnp.max(scores, axis=-1, keepdims=True))
        unnormed = jnp.exp(scores - row_max)
        totals = lax.optimization_barrier(jnp.sum(unnormed, axis=-1))
        weights = lax.optimization_barrier(unnormed.astype(jnp.bfloat16)).astype(jnp.float32)
        summed = jnp.einsum('kgqw,wkd->qkgd', weights, value_block)
        attended = summed / jnp.transpose(totals, (2, 0, 1))[..., None]
        return attended.reshape(block_rows, HEADS * HEAD_DIM).astype(jnp.bfloat16)
    attended = lax.map(attend_block, jnp.arange(LENGTH // block_rows, dtype=jnp.int32))
    attended = attended.reshape(LENGTH, HEADS * HEAD_DIM)
    group_cols = HEADS_DEV * HEAD_DIM
    mixed_rows = residual.astype(jnp.float32)
    for group_index in range(N_EXP):
        part_cols = attended[:, group_index * group_cols:(group_index + 1) * group_cols]
        part_rows = out_weight[group_index * group_cols:(group_index + 1) * group_cols]
        head_term = jnp.dot(part_cols, part_rows, preferred_element_type=jnp.float32).astype(jnp.bfloat16)
        mixed_rows = mixed_rows + lax.optimization_barrier(head_term).astype(jnp.float32)
    mean_square = lax.optimization_barrier(jnp.mean(mixed_rows * mixed_rows, axis=-1, keepdims=True))
    normed = (mixed_rows * lax.rsqrt(mean_square + 1e-06) * norm_gain).astype(jnp.bfloat16)
    flat_ids = expert_ids.reshape(-1).astype(jnp.int32)
    flat_weight = route_weight.reshape(-1)
    most_rows = N_CTX * N_EXP * CAP

    def per_expert(routed, expert_index):
        hits = flat_ids == expert_index
        chosen = jnp.nonzero(hits, size=most_rows, fill_value=0)[0].astype(jnp.int32)
        valid_rows = (jnp.arange(most_rows) < jnp.sum(hits)).astype(routed.dtype)
        token_index = (chosen // TOP).astype(jnp.int32)
        rows_in = normed[token_index]
        gate_proj = jnp.dot(rows_in, gate_weight[expert_index], preferred_element_type=jnp.float32)
        up_proj = jnp.dot(rows_in, up_weight[expert_index], preferred_element_type=jnp.float32)
        hidden = (jax.nn.silu(gate_proj) * up_proj).astype(jnp.bfloat16)
        expert_out = jnp.dot(hidden, down_weight[expert_index], preferred_element_type=jnp.float32).astype(jnp.bfloat16)
        contrib = expert_out.astype(routed.dtype) * (flat_weight[chosen] * valid_rows)[:, None]
        return (routed.at[token_index].add(contrib), None)
    routed, _ = lax.scan(per_expert, jnp.zeros((LENGTH, D), jnp.float32), jnp.arange(EXPERTS, dtype=jnp.int32))
    return (mixed_rows + routed).astype(jnp.bfloat16)
```

```python
import functools
import math

import jax
import jax.numpy as jnp
from jax import lax
from jax.experimental import pallas as pl
from jax.experimental.pallas import tpu as pltpu
from jax.sharding import PartitionSpec as P

HEADS = 32
KV_HEADS = 4
HEAD_DIM = 128
TOP = 8
QUERY_TILE = 256
KEY_TILE = 256
LOW = -1e30
DENSE_BYTES = 32 * 1024 * 1024


def attention_kernel(
    tile_rows, heads, bounds_ref, q_ref, start_ref, k_ref, v_ref, w_ref, out_ref, m_ref, l_ref, acc_ref
):
    tile = pl.program_id(0)
    first = bounds_ref[0, tile]
    last = bounds_ref[1, tile]
    query_begin = bounds_ref[2, tile]
    scale = math.log2(math.e) / math.sqrt(HEAD_DIM)
    m_ref[...] = jnp.full_like(m_ref, LOW)
    l_ref[...] = jnp.zeros_like(l_ref)
    acc_ref[...] = jnp.zeros_like(acc_ref)
    starts = start_ref[...]
    query_pos = query_begin + lax.broadcasted_iota(jnp.int32, (1, tile_rows), 1)

    @pl.loop(first, last)
    def _(key_tile):
        key_begin = pl.multiple_of(key_tile * KEY_TILE, KEY_TILE)
        keys = k_ref[pl.ds(key_begin, KEY_TILE), :]
        values = v_ref[pl.ds(key_begin, KEY_TILE), :]
        key_pos = key_begin + lax.broadcasted_iota(jnp.int32, (KEY_TILE, 1), 0)
        visible = (key_pos >= starts) & (key_pos <= query_pos)
        for head in range(heads):
            query = q_ref[:, head * HEAD_DIM : (head + 1) * HEAD_DIM]
            scores = lax.dot_general(
                keys, query, (((1,), (1,)), ((), ())), preferred_element_type=jnp.float32
            )
            scores = jnp.where(visible, scores * scale, LOW * 2)
            old_max = m_ref[head : head + 1, :]
            new_max = jnp.maximum(old_max, jnp.max(scores, axis=0, keepdims=True))
            rescale = jnp.exp2(old_max - new_max)
            unnormed = jnp.exp2(scores - new_max)
            l_ref[head : head + 1, :] = l_ref[head : head + 1, :] * rescale + jnp.sum(
                unnormed, axis=0, keepdims=True
            )
            m_ref[head : head + 1, :] = new_max
            gained = lax.dot_general(
                values,
                unnormed.astype(jnp.bfloat16),
                (((0,), (0,)), ((), ())),
                preferred_element_type=jnp.float32,
            )
            rows = slice(head * HEAD_DIM, (head + 1) * HEAD_DIM)
            acc_ref[rows, :] = acc_ref[rows, :] * rescale + gained

    for head in range(heads):
        rows = slice(head * HEAD_DIM, (head + 1) * HEAD_DIM)
        acc_ref[rows, :] = acc_ref[rows, :] / l_ref[head : head + 1, :]
    attended = acc_ref[...].T.astype(jnp.bfloat16)
    out_ref[...] = jnp.dot(attended, w_ref[...], preferred_element_type=jnp.float32).astype(
        jnp.bfloat16
    )


def attend(queries, starts, bounds, keys, values, out_weight):
    rows, columns = queries.shape
    heads = columns // HEAD_DIM
    width = out_weight.shape[1]
    tile = min(QUERY_TILE, rows)
    whole = lambda i, bounds: (0, 0)
    return pl.pallas_call(
        functools.partial(attention_kernel, tile, heads),
        out_shape=jax.ShapeDtypeStruct((rows, width), jnp.bfloat16),
        grid_spec=pltpu.PrefetchScalarGridSpec(
            num_scalar_prefetch=1,
            grid=(rows // tile,),
            in_specs=[
                pl.BlockSpec((tile, columns), lambda i, bounds: (i, 0)),
                pl.BlockSpec((1, tile), lambda i, bounds: (0, i)),
                pl.BlockSpec(keys.shape, whole),
                pl.BlockSpec(values.shape, whole),
                pl.BlockSpec(out_weight.shape, whole),
            ],
            out_specs=pl.BlockSpec((tile, width), lambda i, bounds: (i, 0)),
            scratch_shapes=[
                pltpu.VMEM((heads, tile), jnp.float32),
                pltpu.VMEM((heads, tile), jnp.float32),
                pltpu.VMEM((columns, tile), jnp.float32),
            ],
        ),
        compiler_params=pltpu.CompilerParams(vmem_limit_bytes=48 * 1024 * 1024),
    )(bounds, queries, starts, keys, values, out_weight)


def gather_rows(rows):
    return lax.all_gather(rows, ("ctx", "exp"), axis=0, tiled=True)


def scatter_sum(partial):
    return lax.psum_scatter(partial, ("ctx", "exp"), scatter_dimension=0, tiled=True)


def route_slots(expert_ids, route_weight, expert_count):
    own_rows = expert_ids.shape[0]
    experts = jnp.arange(expert_count, dtype=jnp.int32)
    route_table = jnp.sum(
        jnp.where(experts[:, None, None] == expert_ids[None], route_weight[None], 0.0), axis=-1
    )
    my_route = lax.all_to_all(
        route_table, ("ctx", "exp"), split_axis=0, concat_axis=0, tiled=True
    )
    capacity = 2 * own_rows * TOP // expert_count
    hits = my_route > 0
    slot = jnp.cumsum(hits.astype(jnp.int32), axis=1) - 1
    picked = hits[:, None, :] & (
        slot[:, None, :] == jnp.arange(capacity, dtype=jnp.int32)[None, :, None]
    )
    pick = picked.astype(jnp.bfloat16)
    slot_weight = jnp.sum(jnp.where(picked, my_route[:, None, :], 0.0), axis=-1)
    return pick, slot_weight


def apply_expert(arrived, gate_weight, up_weight, down_weight):
    gate_proj = jnp.dot(arrived, gate_weight[0], preferred_element_type=jnp.float32)
    up_proj = jnp.dot(arrived, up_weight[0], preferred_element_type=jnp.float32)
    hidden = (jax.nn.silu(gate_proj) * up_proj).astype(jnp.bfloat16)
    return jnp.dot(hidden, down_weight[0], preferred_element_type=jnp.float32)


def dense_experts(normed, pick, slot_weight, gate_weight, up_weight, down_weight):
    expert_count, capacity, own_rows = pick.shape
    width = normed.shape[1]
    everyone = gather_rows(normed).reshape(expert_count, own_rows, width)
    arrived = jnp.einsum(
        "bsr,brd->bsd", pick, everyone, preferred_element_type=jnp.bfloat16
    ).reshape(-1, width)
    produced = apply_expert(arrived, gate_weight, up_weight, down_weight)
    weighted = (produced * slot_weight.reshape(-1, 1)).astype(jnp.bfloat16)
    partial = jnp.einsum(
        "bsr,bsd->brd",
        pick,
        weighted.reshape(expert_count, capacity, width),
        preferred_element_type=jnp.bfloat16,
    ).reshape(-1, width)
    return scatter_sum(partial).astype(jnp.float32)


def slot_experts(
    normed, expert_ids, route_weight, gate_weight, up_weight, down_weight, expert_count
):
    own_rows, width = normed.shape
    capacity = 2 * own_rows * TOP // expert_count
    flat_ids = expert_ids.reshape(-1)
    experts = jnp.arange(expert_count, dtype=jnp.int32)
    onehot = (flat_ids[:, None] == experts[None, :]).astype(jnp.int32)
    slot_index = jnp.sum(jnp.cumsum(onehot, axis=0) * onehot, axis=1) - 1
    outgoing = (
        jnp.zeros((expert_count, capacity, width), jnp.bfloat16)
        .at[flat_ids, slot_index]
        .set(jnp.repeat(normed, TOP, axis=0))
    )
    swap = functools.partial(
        lax.all_to_all, axis_name=("ctx", "exp"), split_axis=0, concat_axis=0, tiled=True
    )
    arrived = swap(outgoing)
    produced = apply_expert(arrived.reshape(-1, width), gate_weight, up_weight, down_weight)
    returned = swap(produced.astype(jnp.bfloat16).reshape(arrived.shape))
    fetched = returned[flat_ids, slot_index].astype(jnp.float32)
    fetched = fetched * route_weight.reshape(-1)[:, None]
    return jnp.sum(fetched.reshape(own_rows, TOP, width), axis=1)


def shards(
    residual,
    queries,
    key_rows,
    value_rows,
    segment_ids,
    out_weight,
    norm_gain,
    expert_ids,
    route_weight,
    gate_weight,
    up_weight,
    down_weight,
):
    ctx_rows = queries.shape[0]
    local_heads = queries.shape[1] // HEAD_DIM
    group_size = HEADS // KV_HEADS
    exp_index = lax.axis_index("exp")
    ctx_index = lax.axis_index("ctx")
    expert_count = lax.axis_size("ctx") * lax.axis_size("exp")
    kv_index = exp_index * local_heads // group_size
    my_keys = lax.dynamic_slice_in_dim(key_rows, kv_index * HEAD_DIM, HEAD_DIM, 1)
    my_values = lax.dynamic_slice_in_dim(value_rows, kv_index * HEAD_DIM, HEAD_DIM, 1)
    both = lax.all_gather(
        jnp.concatenate([my_keys, my_values], axis=1), "ctx", axis=0, tiled=True
    )
    all_segs = lax.all_gather(segment_ids, "ctx", axis=0, tiled=True)

    own_rows = residual.shape[0]
    if expert_count * own_rows * residual.shape[1] * 2 <= DENSE_BYTES:
        pick, slot_weight = route_slots(expert_ids, route_weight, expert_count)

    starts = jnp.sum((all_segs[:, None] < segment_ids[None, :]).astype(jnp.int32), axis=0)
    tile = min(QUERY_TILE, ctx_rows)
    begins = ctx_index * ctx_rows + jnp.arange(ctx_rows // tile, dtype=jnp.int32) * tile
    bounds = jnp.stack([starts[::tile] // KEY_TILE, (begins + tile - 1) // KEY_TILE + 1, begins])
    head_terms = attend(
        queries,
        starts.reshape(1, -1),
        bounds.astype(jnp.int32),
        both[:, :HEAD_DIM],
        both[:, HEAD_DIM:],
        out_weight,
    )
    attention_sum = lax.psum_scatter(
        head_terms, "exp", scatter_dimension=0, tiled=True
    ).astype(jnp.float32)
    mixed_rows = residual.astype(jnp.float32) + attention_sum
    mean_square = jnp.mean(mixed_rows * mixed_rows, axis=-1, keepdims=True)
    normed = (mixed_rows * lax.rsqrt(mean_square + 1e-06) * norm_gain).astype(jnp.bfloat16)
    width = normed.shape[1]

    if expert_count * own_rows * width * 2 <= DENSE_BYTES:
        routed = dense_experts(normed, pick, slot_weight, gate_weight, up_weight, down_weight)
    else:
        routed = slot_experts(
            normed, expert_ids, route_weight, gate_weight, up_weight, down_weight, expert_count
        )
    return (mixed_rows + routed).astype(jnp.bfloat16)


def solution(mesh):
    return jax.shard_map(
        shards,
        mesh=mesh,
        in_specs=(
            P(("ctx", "exp"), None),
            P("ctx", "exp"),
            P("ctx", None),
            P("ctx", None),
            P("ctx"),
            P("exp", None),
            P(),
            P(("ctx", "exp"), None),
            P(("ctx", "exp"), None),
            P(("ctx", "exp"), None, None),
            P(("ctx", "exp"), None, None),
            P(("ctx", "exp"), None, None),
        ),
        out_specs=P(("ctx", "exp"), None),
        check_vma=False,
    )
```

```python
import functools
import math

import jax
import jax.numpy as jnp
from jax import lax
from jax.experimental import pallas as pl
from jax.experimental.pallas import tpu as pltpu
from jax.sharding import PartitionSpec as P

HEADS = 32
KV_HEADS = 4
HEAD_DIM = 128
TOP = 8
QUERY_TILE = 256
KEY_TILE = 256
LOW = -1e30
BITS = 5
MESH = pl.DeviceIdType.MESH
ORDERS = ((4, 1, 0, 3, 2), (4, 0, 3, 1, 2), (4, 3, 1, 0, 2), (4, 1, 3, 0, 2)) * 2
EXP_ORDERS = ((4, 3, 2),) * 4


def attention_kernel(
    tile_rows, heads, bounds_ref, q_ref, start_ref, k_ref, v_ref, w_ref, out_ref, m_ref, l_ref, acc_ref
):
    tile = pl.program_id(0)
    first = bounds_ref[0, tile]
    last = bounds_ref[1, tile]
    query_begin = bounds_ref[2, tile]
    scale = math.log2(math.e) / math.sqrt(HEAD_DIM)
    m_ref[...] = jnp.full_like(m_ref, LOW)
    l_ref[...] = jnp.zeros_like(l_ref)
    acc_ref[...] = jnp.zeros_like(acc_ref)
    starts = start_ref[...]
    query_pos = query_begin + lax.broadcasted_iota(jnp.int32, (1, tile_rows), 1)

    @pl.loop(first, last)
    def _(key_tile):
        key_begin = pl.multiple_of(key_tile * KEY_TILE, KEY_TILE)
        keys = k_ref[pl.ds(key_begin, KEY_TILE), :]
        values = v_ref[pl.ds(key_begin, KEY_TILE), :]
        key_pos = key_begin + lax.broadcasted_iota(jnp.int32, (KEY_TILE, 1), 0)
        visible = (key_pos >= starts) & (key_pos <= query_pos)
        for head in range(heads):
            query = q_ref[:, head * HEAD_DIM : (head + 1) * HEAD_DIM]
            scores = lax.dot_general(
                keys, query, (((1,), (1,)), ((), ())), preferred_element_type=jnp.float32
            )
            scores = jnp.where(visible, scores * scale, LOW * 2)
            old_max = m_ref[head : head + 1, :]
            new_max = jnp.maximum(old_max, jnp.max(scores, axis=0, keepdims=True))
            rescale = jnp.exp2(old_max - new_max)
            unnormed = jnp.exp2(scores - new_max)
            l_ref[head : head + 1, :] = l_ref[head : head + 1, :] * rescale + jnp.sum(
                unnormed, axis=0, keepdims=True
            )
            m_ref[head : head + 1, :] = new_max
            gained = lax.dot_general(
                values,
                unnormed.astype(jnp.bfloat16),
                (((0,), (0,)), ((), ())),
                preferred_element_type=jnp.float32,
            )
            rows = slice(head * HEAD_DIM, (head + 1) * HEAD_DIM)
            acc_ref[rows, :] = acc_ref[rows, :] * rescale + gained

    for head in range(heads):
        rows = slice(head * HEAD_DIM, (head + 1) * HEAD_DIM)
        acc_ref[rows, :] = acc_ref[rows, :] / l_ref[head : head + 1, :]
    attended = acc_ref[...].T.astype(jnp.bfloat16)
    out_ref[...] = jnp.dot(attended, w_ref[...], preferred_element_type=jnp.float32).astype(
        jnp.bfloat16
    )


def attend(queries, starts, bounds, keys, values, out_weight):
    rows, columns = queries.shape
    heads = columns // HEAD_DIM
    width = out_weight.shape[1]
    tile = min(QUERY_TILE, rows)
    whole = lambda i, bounds: (0, 0)
    return pl.pallas_call(
        functools.partial(attention_kernel, tile, heads),
        out_shape=jax.ShapeDtypeStruct((rows, width), jnp.bfloat16),
        grid_spec=pltpu.PrefetchScalarGridSpec(
            num_scalar_prefetch=1,
            grid=(rows // tile,),
            in_specs=[
                pl.BlockSpec((tile, columns), lambda i, bounds: (i, 0)),
                pl.BlockSpec((1, tile), lambda i, bounds: (0, i)),
                pl.BlockSpec(keys.shape, whole),
                pl.BlockSpec(values.shape, whole),
                pl.BlockSpec(out_weight.shape, whole),
            ],
            out_specs=pl.BlockSpec((tile, width), lambda i, bounds: (i, 0)),
            scratch_shapes=[
                pltpu.VMEM((heads, tile), jnp.float32),
                pltpu.VMEM((heads, tile), jnp.float32),
                pltpu.VMEM((columns, tile), jnp.float32),
            ],
        ),
        compiler_params=pltpu.CompilerParams(vmem_limit_bytes=48 * 1024 * 1024),
    )(bounds, queries, starts, keys, values, out_weight)


def own_bits():
    ctx = lax.axis_index("ctx")
    exp = lax.axis_index("exp")
    return (ctx // 2, ctx % 2, exp // 4, exp // 2 % 2, exp % 2)


def partner(bits, bit):
    b = [1 - value if at == bit else value for at, value in enumerate(bits)]
    return (b[0] * 2 + b[1], b[2] * 4 + b[3] * 2 + b[4])


def waves(chunks, stages):
    for tick in range(stages + 2 * ((chunks - 1) // 4)):
        for j in range(chunks):
            stage = tick - j // 4 * 2
            if 0 <= stage < stages:
                yield j, stage


def greet(bits, active):
    barrier = pltpu.get_barrier_semaphore()
    for bit in active:
        pl.semaphore_signal(
            barrier, inc=1, device_id=partner(bits, bit), device_id_type=MESH
        )
    pl.semaphore_wait(barrier, len(active))


def gather_kernel(rows_ref, out_ref, local_sem, send_sem, recv_sem):
    bits = own_bits()
    chunks = len(ORDERS)
    chunk = rows_ref.shape[1] // chunks
    greet(bits, range(BITS))
    local = pltpu.make_async_copy(rows_ref, out_ref.at[bits], local_sem)
    local.start()
    local.wait()
    copies = {}

    def begin(j, stage):
        order = ORDERS[j][::-1]
        held = order[:stage]
        index = tuple(slice(None) if at in held else bits[at] for at in range(BITS))
        part = out_ref.at[index + (slice(None), pl.ds(j * chunk, chunk))]
        copies[j, stage] = pltpu.make_async_remote_copy(
            src_ref=part,
            dst_ref=part,
            send_sem=send_sem.at[j, stage],
            recv_sem=recv_sem.at[j, stage],
            device_id=partner(bits, order[stage]),
            device_id_type=MESH,
        )
        copies[j, stage].start()

    for j in range(chunks):
        begin(j, 0)
    for j, stage in waves(chunks, BITS):
        copies[j, stage].wait_recv()
        if stage + 1 < BITS:
            begin(j, stage + 1)
    for copy in copies.values():
        copy.wait_send()


def gather_rows(rows):
    return pl.pallas_call(
        gather_kernel,
        out_shape=jax.ShapeDtypeStruct((2,) * BITS + rows.shape, rows.dtype),
        in_specs=[pl.BlockSpec(memory_space=pl.ANY)],
        out_specs=pl.BlockSpec(memory_space=pl.ANY),
        scratch_shapes=[
            pltpu.SemaphoreType.DMA,
            pltpu.SemaphoreType.DMA((len(ORDERS), BITS)),
            pltpu.SemaphoreType.DMA((len(ORDERS), BITS)),
        ],
        compiler_params=pltpu.CompilerParams(collective_id=0, has_side_effects=True),
    )(rows)


def scatter_kernel(orders, partial_ref, out_ref, *scratch):
    chunks = len(orders)
    stages = len(orders[0])
    active = sorted(orders[0])
    landing = scratch[:stages]
    send_sem, recv_sem = scratch[stages:]
    bits = own_bits()
    chunk = out_ref.shape[1] // chunks
    greet(bits, active)
    copies = {}

    def held_ref(j, stage):
        if stage == 0:
            return lambda index: partial_ref.at[index + (slice(None), pl.ds(j * chunk, chunk))]
        return lambda index: landing[stage - 1].at[(j,) + index]

    def half(j, stage, value):
        remaining = [at for at in active if at not in orders[j][:stage]]
        bit = orders[j][stage]
        return tuple(value if at == bit else slice(None) for at in remaining)

    def begin(j, stage):
        bit = orders[j][stage]
        copies[j, stage] = pltpu.make_async_remote_copy(
            src_ref=held_ref(j, stage)(half(j, stage, 1 - bits[bit])),
            dst_ref=landing[stage].at[j],
            send_sem=send_sem.at[j, stage],
            recv_sem=recv_sem.at[j, stage],
            device_id=partner(bits, bit),
            device_id_type=MESH,
        )
        copies[j, stage].start()

    def add(j, stage):
        mine = held_ref(j, stage)
        bit = orders[j][stage]
        remaining = [at for at in active if at not in orders[j][:stage]]
        arrived = landing[stage]
        left = stages - 1 - stage

        @pl.loop(0, 2**left)
        def _(i):
            place = tuple(i // 2 ** (left - 1 - k) % 2 for k in range(left))
            spot = list(place)
            spot.insert(remaining.index(bit), bits[bit])
            total = arrived[(j,) + place].astype(jnp.float32) + mine(tuple(spot))[
                ...
            ].astype(jnp.float32)
            if stage + 1 == stages:
                out_ref[:, j * chunk : (j + 1) * chunk] = total.astype(out_ref.dtype)
            else:
                arrived[(j,) + place] = total.astype(arrived.dtype)

    for j in range(chunks):
        begin(j, 0)
    for j, stage in waves(chunks, stages):
        copies[j, stage].wait_recv()
        add(j, stage)
        if stage + 1 < stages:
            begin(j, stage + 1)
    for copy in copies.values():
        copy.wait_send()


def scatter_sum(partial, orders, collective_id):
    rows, width = partial.shape
    chunks = len(orders)
    stages = len(orders[0])
    own_rows = rows // 2**stages
    return pl.pallas_call(
        functools.partial(scatter_kernel, orders),
        out_shape=jax.ShapeDtypeStruct((own_rows, width), partial.dtype),
        in_specs=[pl.BlockSpec(memory_space=pltpu.VMEM)],
        out_specs=pl.BlockSpec(memory_space=pltpu.VMEM),
        scratch_shapes=[
            pltpu.VMEM(
                (chunks,) + (2,) * (stages - 1 - stage) + (own_rows, width // chunks), partial.dtype
            )
            for stage in range(stages)
        ]
        + [
            pltpu.SemaphoreType.DMA((chunks, stages)),
            pltpu.SemaphoreType.DMA((chunks, stages)),
        ],
        compiler_params=pltpu.CompilerParams(
            collective_id=collective_id, has_side_effects=True, vmem_limit_bytes=52 * 1024 * 1024
        ),
    )(partial.reshape((2,) * stages + (own_rows, width)))


def route_slots(expert_ids, route_weight, expert_count):
    own_rows = expert_ids.shape[0]
    experts = jnp.arange(expert_count, dtype=jnp.int32)
    route_table = jnp.sum(
        jnp.where(experts[:, None, None] == expert_ids[None], route_weight[None], 0.0), axis=-1
    )
    my_route = lax.all_to_all(
        route_table, ("ctx", "exp"), split_axis=0, concat_axis=0, tiled=True
    )
    capacity = 2 * own_rows * TOP // expert_count
    hits = my_route > 0
    slot = jnp.cumsum(hits.astype(jnp.int32), axis=1) - 1
    picked = hits[:, None, :] & (
        slot[:, None, :] == jnp.arange(capacity, dtype=jnp.int32)[None, :, None]
    )
    pick = picked.astype(jnp.bfloat16)
    slot_weight = jnp.sum(jnp.where(picked, my_route[:, None, :], 0.0), axis=-1)
    return pick, slot_weight


def apply_expert(arrived, gate_weight, up_weight, down_weight):
    gate_proj = jnp.dot(arrived, gate_weight[0], preferred_element_type=jnp.float32)
    up_proj = jnp.dot(arrived, up_weight[0], preferred_element_type=jnp.float32)
    hidden = (jax.nn.silu(gate_proj) * up_proj).astype(jnp.bfloat16)
    return jnp.dot(hidden, down_weight[0], preferred_element_type=jnp.float32)


def dense_experts(normed, pick, slot_weight, gate_weight, up_weight, down_weight):
    expert_count, capacity, own_rows = pick.shape
    width = normed.shape[1]
    everyone = gather_rows(normed).reshape(expert_count, own_rows, width)
    arrived = jnp.einsum(
        "bsr,brd->bsd", pick, everyone, preferred_element_type=jnp.bfloat16
    ).reshape(-1, width)
    produced = apply_expert(arrived, gate_weight, up_weight, down_weight)
    weighted = (produced * slot_weight.reshape(-1, 1)).astype(jnp.bfloat16)
    partial = jnp.einsum(
        "bsr,bsd->brd",
        pick,
        weighted.reshape(expert_count, capacity, width),
        preferred_element_type=jnp.bfloat16,
    ).reshape(-1, width)
    return scatter_sum(partial, ORDERS, 1).astype(jnp.float32)


def slot_experts(
    normed, expert_ids, route_weight, gate_weight, up_weight, down_weight, expert_count
):
    own_rows, width = normed.shape
    capacity = 2 * own_rows * TOP // expert_count
    flat_ids = expert_ids.reshape(-1)
    experts = jnp.arange(expert_count, dtype=jnp.int32)
    onehot = (flat_ids[:, None] == experts[None, :]).astype(jnp.int32)
    slot_index = jnp.sum(jnp.cumsum(onehot, axis=0) * onehot, axis=1) - 1
    outgoing = (
        jnp.zeros((expert_count, capacity, width), jnp.bfloat16)
        .at[flat_ids, slot_index]
        .set(jnp.repeat(normed, TOP, axis=0))
    )
    swap = functools.partial(
        lax.all_to_all, axis_name=("ctx", "exp"), split_axis=0, concat_axis=0, tiled=True
    )
    arrived = swap(outgoing)
    produced = apply_expert(arrived.reshape(-1, width), gate_weight, up_weight, down_weight)
    returned = swap(produced.astype(jnp.bfloat16).reshape(arrived.shape))
    fetched = returned[flat_ids, slot_index].astype(jnp.float32)
    fetched = fetched * route_weight.reshape(-1)[:, None]
    return jnp.sum(fetched.reshape(own_rows, TOP, width), axis=1)


def shards(
    residual,
    queries,
    key_rows,
    value_rows,
    segment_ids,
    out_weight,
    norm_gain,
    expert_ids,
    route_weight,
    gate_weight,
    up_weight,
    down_weight,
):
    ctx_rows = queries.shape[0]
    local_heads = queries.shape[1] // HEAD_DIM
    group_size = HEADS // KV_HEADS
    exp_index = lax.axis_index("exp")
    ctx_index = lax.axis_index("ctx")
    expert_count = lax.axis_size("ctx") * lax.axis_size("exp")
    kv_index = exp_index * local_heads // group_size
    my_keys = lax.dynamic_slice_in_dim(key_rows, kv_index * HEAD_DIM, HEAD_DIM, 1)
    my_values = lax.dynamic_slice_in_dim(value_rows, kv_index * HEAD_DIM, HEAD_DIM, 1)
    both = lax.all_gather(
        jnp.concatenate([my_keys, my_values], axis=1), "ctx", axis=0, tiled=True
    )
    all_segs = lax.all_gather(segment_ids, "ctx", axis=0, tiled=True)

    own_rows = residual.shape[0]
    dense = (lax.axis_size("ctx"), lax.axis_size("exp")) == (4, 8)
    if dense:
        pick, slot_weight = route_slots(expert_ids, route_weight, expert_count)

    starts = jnp.sum((all_segs[:, None] < segment_ids[None, :]).astype(jnp.int32), axis=0)
    if dense:
        starts, pick, slot_weight = lax.optimization_barrier((starts, pick, slot_weight))
    tile = min(QUERY_TILE, ctx_rows)
    begins = ctx_index * ctx_rows + jnp.arange(ctx_rows // tile, dtype=jnp.int32) * tile
    bounds = jnp.stack([starts[::tile] // KEY_TILE, (begins + tile - 1) // KEY_TILE + 1, begins])
    head_terms = attend(
        queries,
        starts.reshape(1, -1),
        bounds.astype(jnp.int32),
        both[:, :HEAD_DIM],
        both[:, HEAD_DIM:],
        out_weight,
    )
    if dense:
        attention_sum = scatter_sum(head_terms, EXP_ORDERS, 2).astype(jnp.float32)
    else:
        attention_sum = lax.psum_scatter(
            head_terms, "exp", scatter_dimension=0, tiled=True
        ).astype(jnp.float32)
    mixed_rows = residual.astype(jnp.float32) + attention_sum
    mean_square = jnp.mean(mixed_rows * mixed_rows, axis=-1, keepdims=True)
    normed = (mixed_rows * lax.rsqrt(mean_square + 1e-06) * norm_gain).astype(jnp.bfloat16)
    width = normed.shape[1]

    if dense:
        routed = dense_experts(normed, pick, slot_weight, gate_weight, up_weight, down_weight)
    else:
        routed = slot_experts(
            normed, expert_ids, route_weight, gate_weight, up_weight, down_weight, expert_count
        )
    return (mixed_rows + routed).astype(jnp.bfloat16)


def solution(mesh):
    return jax.shard_map(
        shards,
        mesh=mesh,
        in_specs=(
            P(("ctx", "exp"), None),
            P("ctx", "exp"),
            P("ctx", None),
            P("ctx", None),
            P("ctx"),
            P("exp", None),
            P(),
            P(("ctx", "exp"), None),
            P(("ctx", "exp"), None),
            P(("ctx", "exp"), None, None),
            P(("ctx", "exp"), None, None),
            P(("ctx", "exp"), None, None),
        ),
        out_specs=P(("ctx", "exp"), None),
        check_vma=False,
    )
```

```python
import functools
import math

import jax
import jax.numpy as jnp
from jax import lax
from jax.experimental import pallas as pl
from jax.experimental.pallas import tpu as pltpu
from jax.sharding import PartitionSpec as P

HEADS = 32
KV_HEADS = 4
HEAD_DIM = 128
TOP = 8
QUERY_TILE = 256
KEY_TILE = 256
LOW = -1e30
BITS = 5
MESH = pl.DeviceIdType.MESH
ORDERS = ((4, 1, 0, 3, 2), (4, 0, 3, 1, 2), (4, 3, 1, 0, 2), (4, 1, 3, 0, 2)) * 2
EXP_ORDERS = ((4, 3, 2),) * 4


def attention_kernel(
    tile_rows, heads, bounds_ref, q_ref, start_ref, k_ref, v_ref, w_ref, out_ref, m_ref, l_ref, acc_ref
):
    tile = pl.program_id(0)
    first = bounds_ref[0, tile]
    last = bounds_ref[1, tile]
    query_begin = bounds_ref[2, tile]
    scale = math.log2(math.e) / math.sqrt(HEAD_DIM)
    m_ref[...] = jnp.full_like(m_ref, LOW)
    l_ref[...] = jnp.zeros_like(l_ref)
    acc_ref[...] = jnp.zeros_like(acc_ref)
    starts = start_ref[...]
    query_pos = query_begin + lax.broadcasted_iota(jnp.int32, (1, tile_rows), 1)

    @pl.loop(first, last)
    def _(key_tile):
        key_begin = pl.multiple_of(key_tile * KEY_TILE, KEY_TILE)
        keys = k_ref[pl.ds(key_begin, KEY_TILE), :]
        values = v_ref[pl.ds(key_begin, KEY_TILE), :]
        key_pos = key_begin + lax.broadcasted_iota(jnp.int32, (KEY_TILE, 1), 0)
        visible = (key_pos >= starts) & (key_pos <= query_pos)
        scores = [
            lax.dot_general(
                keys,
                q_ref[:, head * HEAD_DIM : (head + 1) * HEAD_DIM],
                (((1,), (1,)), ((), ())),
                preferred_element_type=jnp.float32,
            )
            for head in range(heads)
        ]
        scores = [jnp.where(visible, part * scale, LOW * 2) for part in scores]
        old_max = m_ref[...]
        old_total = l_ref[...]
        new_max = jnp.maximum(
            old_max,
            jnp.concatenate([jnp.max(part, axis=0, keepdims=True) for part in scores], axis=0),
        )
        rescale = jnp.exp2(old_max - new_max)
        unnormed = [
            jnp.exp2(part - new_max[head : head + 1, :]) for head, part in enumerate(scores)
        ]
        gained = [
            lax.dot_general(
                values,
                part.astype(jnp.bfloat16),
                (((0,), (0,)), ((), ())),
                preferred_element_type=jnp.float32,
            )
            for part in unnormed
        ]
        m_ref[...] = new_max
        l_ref[...] = old_total * rescale + jnp.concatenate(
            [jnp.sum(part, axis=0, keepdims=True) for part in unnormed], axis=0
        )
        for head in range(heads):
            rows = slice(head * HEAD_DIM, (head + 1) * HEAD_DIM)
            acc_ref[rows, :] = acc_ref[rows, :] * rescale[head : head + 1, :] + gained[head]

    for head in range(heads):
        rows = slice(head * HEAD_DIM, (head + 1) * HEAD_DIM)
        acc_ref[rows, :] = acc_ref[rows, :] / l_ref[head : head + 1, :]
    attended = acc_ref[...].T.astype(jnp.bfloat16)
    out_ref[...] = jnp.dot(attended, w_ref[...], preferred_element_type=jnp.float32).astype(
        jnp.bfloat16
    )


def attend(queries, starts, bounds, keys, values, out_weight):
    rows, columns = queries.shape
    heads = columns // HEAD_DIM
    width = out_weight.shape[1]
    tile = min(QUERY_TILE, rows)
    whole = lambda i, bounds: (0, 0)
    return pl.pallas_call(
        functools.partial(attention_kernel, tile, heads),
        out_shape=jax.ShapeDtypeStruct((rows, width), jnp.bfloat16),
        grid_spec=pltpu.PrefetchScalarGridSpec(
            num_scalar_prefetch=1,
            grid=(rows // tile,),
            in_specs=[
                pl.BlockSpec((tile, columns), lambda i, bounds: (i, 0)),
                pl.BlockSpec((1, tile), lambda i, bounds: (0, i)),
                pl.BlockSpec(keys.shape, whole),
                pl.BlockSpec(values.shape, whole),
                pl.BlockSpec(out_weight.shape, whole),
            ],
            out_specs=pl.BlockSpec((tile, width), lambda i, bounds: (i, 0)),
            scratch_shapes=[
                pltpu.VMEM((heads, tile), jnp.float32),
                pltpu.VMEM((heads, tile), jnp.float32),
                pltpu.VMEM((columns, tile), jnp.float32),
            ],
        ),
        compiler_params=pltpu.CompilerParams(vmem_limit_bytes=48 * 1024 * 1024),
    )(bounds, queries, starts, keys, values, out_weight)


def own_bits():
    ctx = lax.axis_index("ctx")
    exp = lax.axis_index("exp")
    return (ctx // 2, ctx % 2, exp // 4, exp // 2 % 2, exp % 2)


def partner(bits, bit):
    b = [1 - value if at == bit else value for at, value in enumerate(bits)]
    return (b[0] * 2 + b[1], b[2] * 4 + b[3] * 2 + b[4])


def waves(chunks, stages):
    for tick in range(stages + 2 * ((chunks - 1) // 4)):
        for j in range(chunks):
            stage = tick - j // 4 * 2
            if 0 <= stage < stages:
                yield j, stage


def greet(bits, active):
    barrier = pltpu.get_barrier_semaphore()
    for bit in active:
        pl.semaphore_signal(
            barrier, inc=1, device_id=partner(bits, bit), device_id_type=MESH
        )
    pl.semaphore_wait(barrier, len(active))


def gather_kernel(rows_ref, out_ref, local_sem, send_sem, recv_sem):
    bits = own_bits()
    chunks = len(ORDERS)
    chunk = rows_ref.shape[1] // chunks
    greet(bits, range(BITS))
    local = pltpu.make_async_copy(rows_ref, out_ref.at[bits], local_sem)
    local.start()
    local.wait()
    copies = {}

    def begin(j, stage):
        order = ORDERS[j][::-1]
        held = order[:stage]
        index = tuple(slice(None) if at in held else bits[at] for at in range(BITS))
        part = out_ref.at[index + (slice(None), pl.ds(j * chunk, chunk))]
        copies[j, stage] = pltpu.make_async_remote_copy(
            src_ref=part,
            dst_ref=part,
            send_sem=send_sem.at[j, stage],
            recv_sem=recv_sem.at[j, stage],
            device_id=partner(bits, order[stage]),
            device_id_type=MESH,
        )
        copies[j, stage].start()

    for j in range(chunks):
        begin(j, 0)
    for j, stage in waves(chunks, BITS):
        copies[j, stage].wait_recv()
        if stage + 1 < BITS:
            begin(j, stage + 1)
    for copy in copies.values():
        copy.wait_send()


def gather_rows(rows):
    return pl.pallas_call(
        gather_kernel,
        out_shape=jax.ShapeDtypeStruct((2,) * BITS + rows.shape, rows.dtype),
        in_specs=[pl.BlockSpec(memory_space=pltpu.VMEM)],
        out_specs=pl.BlockSpec(memory_space=pltpu.VMEM),
        scratch_shapes=[
            pltpu.SemaphoreType.DMA,
            pltpu.SemaphoreType.DMA((len(ORDERS), BITS)),
            pltpu.SemaphoreType.DMA((len(ORDERS), BITS)),
        ],
        compiler_params=pltpu.CompilerParams(
            collective_id=0, has_side_effects=True, vmem_limit_bytes=40 * 1024 * 1024
        ),
    )(rows)


def scatter_kernel(orders, partial_ref, out_ref, *scratch):
    chunks = len(orders)
    stages = len(orders[0])
    active = sorted(orders[0])
    landing = scratch[:stages]
    send_sem, recv_sem = scratch[stages:]
    bits = own_bits()
    chunk = out_ref.shape[1] // chunks
    greet(bits, active)
    copies = {}

    def held_ref(j, stage):
        if stage == 0:
            return lambda index: partial_ref.at[index + (slice(None), pl.ds(j * chunk, chunk))]
        return lambda index: landing[stage - 1].at[(j,) + index]

    def half(j, stage, value):
        remaining = [at for at in active if at not in orders[j][:stage]]
        bit = orders[j][stage]
        return tuple(value if at == bit else slice(None) for at in remaining)

    def begin(j, stage):
        bit = orders[j][stage]
        copies[j, stage] = pltpu.make_async_remote_copy(
            src_ref=held_ref(j, stage)(half(j, stage, 1 - bits[bit])),
            dst_ref=landing[stage].at[j],
            send_sem=send_sem.at[j, stage],
            recv_sem=recv_sem.at[j, stage],
            device_id=partner(bits, bit),
            device_id_type=MESH,
        )
        copies[j, stage].start()

    def add(j, stage):
        mine = held_ref(j, stage)
        bit = orders[j][stage]
        remaining = [at for at in active if at not in orders[j][:stage]]
        arrived = landing[stage]
        left = stages - 1 - stage

        @pl.loop(0, 2**left)
        def _(i):
            place = tuple(i // 2 ** (left - 1 - k) % 2 for k in range(left))
            spot = list(place)
            spot.insert(remaining.index(bit), bits[bit])
            total = arrived[(j,) + place].astype(jnp.float32) + mine(tuple(spot))[
                ...
            ].astype(jnp.float32)
            if stage + 1 == stages:
                out_ref[:, j * chunk : (j + 1) * chunk] = total.astype(out_ref.dtype)
            else:
                arrived[(j,) + place] = total.astype(arrived.dtype)

    for j in range(chunks):
        begin(j, 0)
    for j, stage in waves(chunks, stages):
        copies[j, stage].wait_recv()
        add(j, stage)
        if stage + 1 < stages:
            begin(j, stage + 1)
    for copy in copies.values():
        copy.wait_send()


def scatter_sum(partial, orders, collective_id):
    rows, width = partial.shape
    chunks = len(orders)
    stages = len(orders[0])
    own_rows = rows // 2**stages
    return pl.pallas_call(
        functools.partial(scatter_kernel, orders),
        out_shape=jax.ShapeDtypeStruct((own_rows, width), partial.dtype),
        in_specs=[pl.BlockSpec(memory_space=pltpu.VMEM)],
        out_specs=pl.BlockSpec(memory_space=pltpu.VMEM),
        scratch_shapes=[
            pltpu.VMEM(
                (chunks,) + (2,) * (stages - 1 - stage) + (own_rows, width // chunks), partial.dtype
            )
            for stage in range(stages)
        ]
        + [
            pltpu.SemaphoreType.DMA((chunks, stages)),
            pltpu.SemaphoreType.DMA((chunks, stages)),
        ],
        compiler_params=pltpu.CompilerParams(
            collective_id=collective_id, has_side_effects=True, vmem_limit_bytes=52 * 1024 * 1024
        ),
    )(partial.reshape((2,) * stages + (own_rows, width)))


def route_slots(expert_ids, route_weight, expert_count):
    own_rows = expert_ids.shape[0]
    experts = jnp.arange(expert_count, dtype=jnp.int32)
    route_table = jnp.sum(
        jnp.where(experts[:, None, None] == expert_ids[None], route_weight[None], 0.0), axis=-1
    )
    my_route = lax.all_to_all(
        route_table, ("ctx", "exp"), split_axis=0, concat_axis=0, tiled=True
    )
    capacity = 2 * own_rows * TOP // expert_count
    hits = my_route > 0
    slot = jnp.cumsum(hits.astype(jnp.int32), axis=1) - 1
    picked = hits[:, None, :] & (
        slot[:, None, :] == jnp.arange(capacity, dtype=jnp.int32)[None, :, None]
    )
    pick = picked.astype(jnp.bfloat16)
    slot_weight = jnp.sum(jnp.where(picked, my_route[:, None, :], 0.0), axis=-1)
    return pick, slot_weight


def apply_expert(arrived, gate_weight, up_weight, down_weight):
    gate_proj = jnp.dot(arrived, gate_weight[0], preferred_element_type=jnp.float32)
    up_proj = jnp.dot(arrived, up_weight[0], preferred_element_type=jnp.float32)
    hidden = (jax.nn.silu(gate_proj) * up_proj).astype(jnp.bfloat16)
    return jnp.dot(hidden, down_weight[0], preferred_element_type=jnp.float32)


def dense_experts(normed, pick, slot_weight, gate_weight, up_weight, down_weight):
    expert_count, capacity, own_rows = pick.shape
    width = normed.shape[1]
    everyone = gather_rows(normed).reshape(expert_count, own_rows, width)
    arrived = jnp.einsum(
        "bsr,brd->bsd", pick, everyone, preferred_element_type=jnp.bfloat16
    ).reshape(-1, width)
    produced = apply_expert(arrived, gate_weight, up_weight, down_weight)
    weighted = (produced * slot_weight.reshape(-1, 1)).astype(jnp.bfloat16)
    partial = jnp.einsum(
        "bsr,bsd->brd",
        pick,
        weighted.reshape(expert_count, capacity, width),
        preferred_element_type=jnp.bfloat16,
    ).reshape(-1, width)
    return scatter_sum(partial, ORDERS, 1).astype(jnp.float32)


def slot_experts(
    normed, expert_ids, route_weight, gate_weight, up_weight, down_weight, expert_count
):
    own_rows, width = normed.shape
    capacity = 2 * own_rows * TOP // expert_count
    flat_ids = expert_ids.reshape(-1)
    experts = jnp.arange(expert_count, dtype=jnp.int32)
    onehot = (flat_ids[:, None] == experts[None, :]).astype(jnp.int32)
    slot_index = jnp.sum(jnp.cumsum(onehot, axis=0) * onehot, axis=1) - 1
    outgoing = (
        jnp.zeros((expert_count, capacity, width), jnp.bfloat16)
        .at[flat_ids, slot_index]
        .set(jnp.repeat(normed, TOP, axis=0))
    )
    swap = functools.partial(
        lax.all_to_all, axis_name=("ctx", "exp"), split_axis=0, concat_axis=0, tiled=True
    )
    arrived = swap(outgoing)
    produced = apply_expert(arrived.reshape(-1, width), gate_weight, up_weight, down_weight)
    returned = swap(produced.astype(jnp.bfloat16).reshape(arrived.shape))
    fetched = returned[flat_ids, slot_index].astype(jnp.float32)
    fetched = fetched * route_weight.reshape(-1)[:, None]
    return jnp.sum(fetched.reshape(own_rows, TOP, width), axis=1)


def shards(
    residual,
    queries,
    key_rows,
    value_rows,
    segment_ids,
    out_weight,
    norm_gain,
    expert_ids,
    route_weight,
    gate_weight,
    up_weight,
    down_weight,
):
    ctx_rows = queries.shape[0]
    local_heads = queries.shape[1] // HEAD_DIM
    group_size = HEADS // KV_HEADS
    exp_index = lax.axis_index("exp")
    ctx_index = lax.axis_index("ctx")
    expert_count = lax.axis_size("ctx") * lax.axis_size("exp")
    kv_index = exp_index * local_heads // group_size
    my_keys = lax.dynamic_slice_in_dim(key_rows, kv_index * HEAD_DIM, HEAD_DIM, 1)
    my_values = lax.dynamic_slice_in_dim(value_rows, kv_index * HEAD_DIM, HEAD_DIM, 1)
    both = lax.all_gather(
        jnp.concatenate([my_keys, my_values], axis=1), "ctx", axis=0, tiled=True
    )
    all_segs = lax.all_gather(segment_ids, "ctx", axis=0, tiled=True)

    own_rows = residual.shape[0]
    dense = (lax.axis_size("ctx"), lax.axis_size("exp")) == (4, 8)
    if dense:
        pick, slot_weight = route_slots(expert_ids, route_weight, expert_count)

    starts = jnp.sum((all_segs[:, None] < segment_ids[None, :]).astype(jnp.int32), axis=0)
    if dense:
        starts, pick, slot_weight = lax.optimization_barrier((starts, pick, slot_weight))
    tile = min(QUERY_TILE, ctx_rows)
    begins = ctx_index * ctx_rows + jnp.arange(ctx_rows // tile, dtype=jnp.int32) * tile
    bounds = jnp.stack([starts[::tile] // KEY_TILE, (begins + tile - 1) // KEY_TILE + 1, begins])
    head_terms = attend(
        queries,
        starts.reshape(1, -1),
        bounds.astype(jnp.int32),
        both[:, :HEAD_DIM],
        both[:, HEAD_DIM:],
        out_weight,
    )
    if dense:
        attention_sum = scatter_sum(head_terms, EXP_ORDERS, 2).astype(jnp.float32)
    else:
        attention_sum = lax.psum_scatter(
            head_terms, "exp", scatter_dimension=0, tiled=True
        ).astype(jnp.float32)
    mixed_rows = residual.astype(jnp.float32) + attention_sum
    mean_square = jnp.mean(mixed_rows * mixed_rows, axis=-1, keepdims=True)
    normed = (mixed_rows * lax.rsqrt(mean_square + 1e-06) * norm_gain).astype(jnp.bfloat16)
    width = normed.shape[1]

    if dense:
        routed = dense_experts(normed, pick, slot_weight, gate_weight, up_weight, down_weight)
    else:
        routed = slot_experts(
            normed, expert_ids, route_weight, gate_weight, up_weight, down_weight, expert_count
        )
    return (mixed_rows + routed).astype(jnp.bfloat16)


def solution(mesh):
    return jax.shard_map(
        shards,
        mesh=mesh,
        in_specs=(
            P(("ctx", "exp"), None),
            P("ctx", "exp"),
            P("ctx", None),
            P("ctx", None),
            P("ctx"),
            P("exp", None),
            P(),
            P(("ctx", "exp"), None),
            P(("ctx", "exp"), None),
            P(("ctx", "exp"), None, None),
            P(("ctx", "exp"), None, None),
            P(("ctx", "exp"), None, None),
        ),
        out_specs=P(("ctx", "exp"), None),
        check_vma=False,
    )
```
